256 devices in a mesh: rep: 32 (over y, z_hi, core), fsdp: 8 (over z_lo, x).
Axes of the slice: x: 4, y: 4, z: 8 (z_hi: 4, z_lo: 2; z = z_hi * 2 + z_lo), core: 2. Of those that a mesh axis runs over, the one named last changes fastest.
Arguments:
- activations: bfloat16 [2, 32, 1024, 5120], P(None, 'rep', 'fsdp'), may hold values from -6 to 6
- targets: bfloat16 [2, 32, 1024, 2560], P(None, 'rep', 'fsdp'), may hold values from -6 to 6
- params: bfloat16 [32, 2560, 5120], P('rep', 'fsdp'), may hold values from -6 to 6
- push_weight: bfloat16 [32], P('rep'), may hold values from 0.5 to 2
- peer_codes: int32 [2], replicated, may hold values from 0 to 7
Outputs:
- new_params: bfloat16 [32, 2560, 5120], P('rep', 'fsdp')
- new_weight: bfloat16 [32], P('rep')
The draws below stay inside these ranges and needn't reach their ends.
All inputs are finite; a program needn't handle non-finite values.
Results may differ from the reference program's by a relative error of at most 0.015.
Values may be sent and summed in bfloat16 or wider, within the bound.
A program may use at most 192 MiB of HBM per device.

```python
import math
import jax
import jax.numpy as jnp
from jax import lax

D = 5120
STEPS = 2
EXPS = 4
HW = 2560
REPS = 32
TOKENS = 1024


def steps_of(rng, shape, split, low, largest):
    factor_of, own = 1.0, jax.random.fold_in(rng, 6)
    for dim, blocks in split:
        heights = jnp.exp(jax.random.uniform(jax.random.fold_in(own, dim), (blocks,), jnp.float32, low / len(split), largest / len(split)))
        factor_of = factor_of * jnp.repeat(heights, shape[dim] // blocks).reshape([-1 if axis == dim else 1 for axis in range(len(shape))])
    return factor_of


def bell_draw(rng, extent, spread, most, shards=(), kind=jnp.bfloat16):
    level = steps_of(rng, extent, shards, -0.22, 0.18) if shards else 1.0
    drawn = jax.random.normal(rng, extent, jnp.float32) * spread * level
    return jnp.minimum(jnp.maximum(drawn, -most), most).astype(kind)


def setup_inputs(seed: int = 0) -> dict:
    streams_of = jax.random.split(jax.random.key(seed), 6)
    return {
        "activations": bell_draw(streams_of[0], (STEPS, REPS, TOKENS, D), 1.0, 6.0, ((1, 32), (2, 8))),
        "targets": bell_draw(streams_of[1], (STEPS, REPS, TOKENS, HW), 1.0, 6.0, ((1, 32), (2, 8))),
        "params": bell_draw(streams_of[2], (REPS, HW, D), 1.0, 6.0, ((0, 32), (1, 8))),
        "push_weight": jnp.clip(jnp.exp(math.log(2.0) - 1.3862944 * jax.random.uniform(streams_of[3], (REPS,), jnp.float32) ** steps_of(streams_of[3], (REPS,), ((0, 32),), -0.2, 0.2)), 0.5, 2.0).astype(jnp.bfloat16),
        "peer_codes": jax.random.randint(streams_of[4], (STEPS,), 0, 2 * EXPS).astype(jnp.int32),
    }


def reference(activations, targets, params, push_weight, peer_codes):
    scale = D ** (-0.5)
    moment = jnp.zeros(params.shape, jnp.float32)
    second = jnp.zeros(params.shape, jnp.float32)
    current = params
    weight = push_weight
    for step in range(STEPS):
        count = step + 1

        def replica(items):
            inputs, goal, numer, wval, first_m, second_v = items
            debiased = (numer.astype(jnp.float32) / wval.astype(jnp.float32)).astype(jnp.bfloat16)
            output = jnp.dot(inputs, debiased.T, preferred_element_type=jnp.float32) * scale
            error = ((output - goal.astype(jnp.float32)) / TOKENS).astype(jnp.bfloat16)
            grad = jnp.dot(error.T, inputs, preferred_element_type=jnp.float32) * scale
            first_m = 0.9 * first_m + 0.1 * grad
            second_v = 0.95 * second_v + 0.05 * grad * grad
            update = first_m / (1.0 - 0.9 ** count) / (jnp.sqrt(second_v / (1.0 - 0.95 ** count)) + 0.0001)
            halfway = (numer.astype(jnp.float32) - 0.08 * update).astype(jnp.bfloat16)
            return (halfway, first_m, second_v)
        halfway, moment, second = lax.map(replica, (activations[step], targets[step], current, weight, moment, second))
        code = peer_codes[step].astype(jnp.int32)
        power = (2 ** (code // 2)).astype(jnp.int32)
        offset = jnp.where(code % 2 == 0, power, REPS - power).astype(jnp.int32)
        arrived = jnp.roll(halfway, offset, axis=0)
        current = (0.5 * (halfway.astype(jnp.float32) + arrived.astype(jnp.float32))).astype(jnp.bfloat16)
        weight = (0.5 * (weight.astype(jnp.float32) + jnp.roll(weight, offset, axis=0).astype(jnp.float32))).astype(jnp.bfloat16)
    return (current, weight)
```

```python
import functools

import jax
import jax.numpy as jnp
from jax import lax
from jax.experimental import pallas as pl
from jax.experimental.pallas import tpu as pltpu
from jax.sharding import PartitionSpec as P

MESH = pl.DeviceIdType.MESH
REPS, XS, ZS, YS = 32, 4, 2, 4
TOK, D, HW, ROWS = 128, 5120, 2560, 320
ALL = 1024
SCALE = D**-0.5
WIN = 384
F32, BF16 = jnp.float32, jnp.bfloat16
SLOT = {(0, 0): 0, (0, 1): 1, (-1, 0): 2, (1, 0): 3, (-1, 1): 4, (1, 1): 5, (2, 0): 6, (2, 1): 7}
VMEM_LIMIT = 56 * 1024 * 1024


def place():
    return lax.axis_index("rep"), lax.axis_index("fsdp")


def member(f, dx, dz):
    x, z = lax.rem(f, XS), f // XS
    return lax.rem(z + dz, ZS) * XS + lax.rem(x + dx + XS, XS)


def moved(r, dy, dz):
    y, z, c = r // 8, lax.rem(r // 2, 4), lax.rem(r, 2)
    return lax.rem(y + dy + 8, 4) * 8 + lax.rem(z + dz + 8, 4) * 2 + c


def greet(devices):
    barrier = pltpu.get_barrier_semaphore()
    for device in devices:
        pl.semaphore_signal(barrier, inc=1, device_id=device, device_id_type=MESH)
    pl.semaphore_wait(barrier, len(devices))


class Sender:
    def __init__(self, send_sems, recv_sems):
        self.send_sems, self.recv_sems, self.started = send_sems, recv_sems, []

    def __call__(self, src, dst, device):
        i = len(self.started)
        copy = pltpu.make_async_remote_copy(
            src_ref=src, dst_ref=dst, send_sem=self.send_sems.at[i], recv_sem=self.recv_sems.at[i],
            device_id=device, device_id_type=MESH,
        )
        copy.start()
        self.started.append(copy)
        return copy

    def finish(self):
        for copy in self.started:
            copy.wait_send()


def part(ref, slot, lo, hi):
    return ref.at[pl.ds(slot * TOK + lo, hi - lo)]


def target_window(f):
    return pl.ds(pl.multiple_of(320 * f - 64 * lax.rem(f, 2), 128), WIN)


def send_targets(sender, r, f, src, dst):
    copies = []
    for (dx, dz), _ in SLOT.items():
        if (dx, dz) == (0, 0):
            continue
        to = member(f, dx, dz)
        back = SLOT[(dx if dx == 2 else -dx, dz)]
        copies.append((back, sender(src.at[:, target_window(to)], part(dst, back, 0, TOK), (r, to))))
    return [copy for _, copy in sorted(copies, key=lambda c: c[0])]


def first_kernel(cut, p_ref, w_ref, act_ref, tgt_ref, h_ref, g_ref, a1z_ref, t1_ref,
                 A, Pv, Z, G, T, Tt, send_sems, recv_sems, local):
    r, f = place()
    right, left, across = (r, member(f, 1, 0)), (r, member(f, -1, 0)), (r, member(f, 0, 1))
    act0, act1 = act_ref.at[0, 0], act_ref.at[1, 0]
    load_p = pltpu.make_async_copy(p_ref, Pv, local.at[0])
    load_p.start()
    load_a = pltpu.make_async_copy(act0, part(A, 0, 0, TOK), local.at[1])
    load_a.start()
    load_t = pltpu.make_async_copy(tgt_ref.at[0, 0, :, target_window(f)], part(T, 0, 0, TOK), local.at[2])
    load_t.start()
    load_t1 = pltpu.make_async_copy(tgt_ref.at[1, 0, :, target_window(f)], part(t1_ref, 0, 0, TOK), local.at[3])
    load_t1.start()
    greet([(r, member(f, dx, dz)) for dx, dz in SLOT if (dx, dz) != (0, 0)])
    send = Sender(send_sems, recv_sems)

    def own(lo, hi, slot, device):
        return send(act0.at[pl.ds(lo, hi - lo)], part(A, slot, lo, hi), device)

    def forward(source, slot, lo, hi, device):
        return send(part(A, source, lo, hi), part(A, slot, lo, hi), device)

    half = cut + (TOK - cut) // 32 * 16
    z_low = own(cut, TOK, 1, across)
    x_right = own(0, TOK, 2, right)
    x_left = own(0, TOK, 3, left)
    z_top = own(0, cut, 1, across)
    t_copies = send_targets(send, r, f, tgt_ref.at[0, 0], T)

    load_p.wait()
    inverse = 1.0 / w_ref[0:1, 0:1]

    def debias(i, _):
        rows = pl.ds(pl.multiple_of(i * 32, 32), 32)
        Z[rows, :] = (Pv[rows, :].astype(F32) * inverse).astype(BF16)
        return 0

    lax.fori_loop(0, ROWS // 32, debias, 0)

    def use_pair(k):
        rows = pl.ds(k * 2 * TOK, 2 * TOK)
        Tt[...] = T[rows, :].astype(F32).T
        goal = Tt[pl.ds(pl.multiple_of(64 * lax.rem(f, 2), 64), ROWS), :]

        def along(i, total):
            cols = pl.ds(pl.multiple_of(i * 1024, 1024), 1024)
            return total + lax.dot_general(
                Z[:, cols], A[rows, cols], (((1,), (1,)), ((), ())), preferred_element_type=F32
            )

        output = lax.fori_loop(0, D // 1024, along, jnp.zeros((ROWS, 2 * TOK), F32))
        error = ((output * SCALE - goal) * (1.0 / ALL)).astype(BF16)

        def grad(i, _):
            cols = pl.ds(pl.multiple_of(i * 512, 512), 512)
            new = jnp.dot(error, A[rows, cols], preferred_element_type=F32)
            if k == 0:
                G[:, cols] = new
            elif k < 3:
                G[:, cols] += new
            else:
                total = (G[:, cols] + new) * SCALE
                G[:, cols] = total
            return 0

        lax.fori_loop(0, D // 512, grad, 0)

    z_low.wait_recv()
    b_right = forward(1, 4, cut, TOK, right)
    b_left = forward(1, 5, cut, TOK, left)
    x_right.wait_recv()
    f_right = forward(2, 6, 0, 64, right)
    z_2 = forward(2, 4, 0, cut, across)
    x_left.wait_recv()
    f_left = forward(3, 6, 64, TOK, left)
    z_3 = forward(3, 5, 0, cut, across)
    z_top.wait_recv()
    load_a.wait()
    load_t.wait()
    t_copies[0].wait_recv()
    use_pair(0)
    b_right.wait_recv()
    g_right = forward(4, 7, cut, half, right)
    b_left.wait_recv()
    g_left = forward(5, 7, half, TOK, left)
    t_copies[1].wait_recv()
    t_copies[2].wait_recv()
    use_pair(1)
    f_right.wait_recv()
    z_6 = forward(6, 7, 0, cut, across)
    early = send(act1, a1z_ref, across)
    z_2.wait_recv()
    z_3.wait_recv()
    t_copies[3].wait_recv()
    t_copies[4].wait_recv()
    use_pair(2)
    f_left.wait_recv()
    g_right.wait_recv()
    g_left.wait_recv()
    z_6.wait_recv()
    t_copies[5].wait_recv()
    t_copies[6].wait_recv()
    t1_copies = send_targets(send, r, f, tgt_ref.at[1, 0], t1_ref)
    use_pair(3)
    save_g = pltpu.make_async_copy(G, g_ref, local.at[0])
    save_g.start()

    def update(i, _):
        rows = pl.ds(pl.multiple_of(i * 16, 16), 16)
        grad = G[rows, :]
        Z[rows, :] = (Pv[rows, :].astype(F32) - 0.08 * (grad / (jnp.abs(grad) + 1e-4))).astype(BF16)
        return 0

    lax.fori_loop(0, ROWS // 16, update, 0)
    save_h = pltpu.make_async_copy(Z, h_ref, local.at[1])
    save_h.start()
    early.wait_recv()
    for copy in t1_copies:
        copy.wait_recv()
    load_t1.wait()
    save_g.wait()
    save_h.wait()
    send.finish()


def first_step(params, weight, activations, targets, cut):
    any_space = pl.BlockSpec(memory_space=pl.ANY)
    return pl.pallas_call(
        functools.partial(first_kernel, cut),
        out_shape=(
            jax.ShapeDtypeStruct((ROWS, D), BF16),
            jax.ShapeDtypeStruct((ROWS, D), F32),
            jax.ShapeDtypeStruct((TOK, D), BF16),
            jax.ShapeDtypeStruct((ALL, WIN), BF16),
        ),
        in_specs=[any_space, pl.BlockSpec(memory_space=pltpu.VMEM), any_space, any_space],
        out_specs=(any_space,) * 4,
        scratch_shapes=[
            pltpu.VMEM((ALL, D), BF16),
            pltpu.VMEM((ROWS, D), BF16),
            pltpu.VMEM((ROWS, D), BF16),
            pltpu.VMEM((ROWS, D), F32),
            pltpu.VMEM((ALL, WIN), BF16),
            pltpu.VMEM((WIN, 2 * TOK), F32),
            pltpu.SemaphoreType.DMA((32,)),
            pltpu.SemaphoreType.DMA((32,)),
            pltpu.SemaphoreType.DMA((4,)),
        ],
        compiler_params=pltpu.CompilerParams(
            collective_id=0, has_side_effects=True, vmem_limit_bytes=VMEM_LIMIT
        ),
        name="first_step",
    )(params, weight, activations, targets)


class Push:
    def __init__(self, code, r, f):
        power = 1 << (code // 2)
        offset = power if code % 2 == 0 else -power
        self.f = f
        self.to, self.source = lax.rem(r + offset + REPS, REPS), lax.rem(r - offset + REPS, REPS)
        self.legs = code // 2 in (1, 3)
        self.back = 80 if self.legs else 0
        if self.legs:
            way = -1 if code % 2 == 0 else 1
            dy, dz = (0, way) if code // 2 == 1 else (way, 0)
            self.next, self.last_one = moved(r, dy, dz), moved(r, -dy, -dz)
            self.end = lax.rem(moved(r, -2 * dy, -2 * dz) + offset + REPS, REPS)
            self.start_of_end = moved(self.source, 2 * dy, 2 * dz)

    def partners(self):
        both = [self.to, self.source]
        if self.legs:
            both += [self.next, self.last_one, self.end, self.start_of_end]
        return [(device, self.f) for device in both]


def exchange_kernel(code, cut, h_ref, w_ref, act_ref, a1z_ref, arr_ref, warr_ref, a1_ref,
                    relay, send_sems, recv_sems, local):
    r, f = place()
    right, left, across = (r, member(f, 1, 0)), (r, member(f, -1, 0)), (r, member(f, 0, 1))
    act1 = act_ref.at[1, 0]
    loads = [
        pltpu.make_async_copy(act1, part(a1_ref, 0, 0, TOK), local.at[0]),
        pltpu.make_async_copy(a1z_ref, part(a1_ref, 1, 0, TOK), local.at[1]),
    ]
    for load in loads:
        load.start()
    push = Push(code, r, f)
    greet([right, left] + ([across] if cut else []) + push.partners())
    send = Sender(send_sems, recv_sems)
    back = push.back

    def forward(source, slot, lo, hi, device):
        return send(part(a1_ref, source, lo, hi), part(a1_ref, slot, lo, hi), device)

    if back:
        leg = send(h_ref.at[pl.ds(0, back)], relay.at[0], (push.next, f))
    straight = send(h_ref.at[pl.ds(back, ROWS - back)], arr_ref.at[pl.ds(back, ROWS - back)], (push.to, f))
    weight = send(w_ref, warr_ref, (push.to, f))
    x_right = send(act1, part(a1_ref, 2, 0, TOK), right)
    x_left = send(act1, part(a1_ref, 3, 0, TOK), left)
    b_right = send(a1z_ref.at[pl.ds(cut, TOK - cut)], part(a1_ref, 4, cut, TOK), right)
    b_left = send(a1z_ref.at[pl.ds(cut, TOK - cut)], part(a1_ref, 5, cut, TOK), left)
    half = cut + (TOK - cut) // 32 * 16
    if back:
        leg.wait_recv()
        leg = send(relay.at[0], relay.at[1], (push.next, f))
    x_right.wait_recv()
    f_right = forward(2, 6, 0, 64, right)
    x_left.wait_recv()
    f_left = forward(3, 6, 64, TOK, left)
    ups = []
    if cut:
        ups = [forward(2, 4, 0, cut, across), forward(3, 5, 0, cut, across)]
    if back:
        leg.wait_recv()
        leg = send(relay.at[1], arr_ref.at[pl.ds(0, back)], (push.end, f))
    b_right.wait_recv()
    g_right = forward(4, 7, cut, half, right)
    b_left.wait_recv()
    g_left = forward(5, 7, half, TOK, left)
    f_right.wait_recv()
    f_left.wait_recv()
    if cut:
        ups.append(forward(6, 7, 0, cut, across))
    for copy in [g_right, g_left, *ups, weight, straight] + ([leg] if back else []):
        copy.wait_recv()
    for load in loads:
        load.wait()
    send.finish()


def exchange(code, halfway, weight, activations, a1z):
    any_space = pl.BlockSpec(memory_space=pl.ANY)
    return pl.pallas_call(
        functools.partial(exchange_kernel, code, 64 if code // 2 == 3 else 0),
        out_shape=(
            jax.ShapeDtypeStruct((ROWS, D), BF16),
            jax.ShapeDtypeStruct((8, 128), F32),
            jax.ShapeDtypeStruct((ALL, D), BF16),
        ),
        in_specs=[any_space] * 4,
        out_specs=(any_space,) * 3,
        scratch_shapes=[
            pltpu.VMEM((2, 80, D), BF16),
            pltpu.SemaphoreType.DMA((16,)),
            pltpu.SemaphoreType.DMA((16,)),
            pltpu.SemaphoreType.DMA((2,)),
        ],
        compiler_params=pltpu.CompilerParams(
            collective_id=1 + code, has_side_effects=True, vmem_limit_bytes=VMEM_LIMIT
        ),
        name="exchange",
    )(halfway, weight, activations, a1z)


def second_kernel(code, h_ref, arr_ref, w_ref, warr_ref, a1_ref, t1_ref, g_ref, out_ref, wout_ref,
                  A, Pv, Z, Hv, Arr, G, T, Tt, E, W, Warr, relay, send_sems, recv_sems, local):
    r, f = place()
    chunk = 160
    loads = {}
    for i, (name, src, dst) in enumerate([
        ("h", h_ref, Pv), ("arr", arr_ref, Z), ("t", t1_ref, T),
        ("a0", a1_ref.at[pl.ds(0, 512)], A.at[pl.ds(0, 512)]),
        ("a1", a1_ref.at[pl.ds(512, 512)], A.at[pl.ds(512, 512)]),
        ("g", g_ref, G),
    ]):
        loads[name] = pltpu.make_async_copy(src, dst, local.at[i])
        loads[name].start()
    push = Push(code, r, f)
    back = push.back
    greet(push.partners())
    send = Sender(send_sems, recv_sems)
    W[...] = (0.5 * (w_ref[...] + warr_ref[...])).astype(BF16).astype(F32)
    weight = send(W, Warr, (push.to, f))
    inverse = 1.0 / W[0:1, 0:1]
    loads["h"].wait()
    loads["arr"].wait()

    def average(i, _):
        rows = pl.ds(pl.multiple_of(i * 16, 16), 16)
        new = (0.5 * (Pv[rows, :].astype(F32) + Z[rows, :].astype(F32))).astype(BF16)
        Pv[rows, :] = new
        Z[rows, :] = (new.astype(F32) * inverse).astype(BF16)
        return 0

    lax.fori_loop(0, ROWS // 16, average, 0)
    loads["t"].wait()

    def turn(i, _):
        rows = pl.ds(pl.multiple_of(i * 256, 256), 256)
        Tt[:, rows] = T[rows, :].astype(F32).T
        return 0

    lax.fori_loop(0, ALL // 256, turn, 0)
    shift = 64 * lax.rem(f, 2)
    for name in ("a0", "a1", "g"):
        loads[name].wait()

    def chunk_of(c):
        mine = pl.ds(c * chunk, chunk)
        goals = pl.ds(pl.multiple_of(c * chunk + shift, 32), chunk)

        def errors(k, _):
            rows = pl.ds(pl.multiple_of(k * 256, 256), 256)

            def along(i, total):
                cols = pl.ds(pl.multiple_of(i * 1024, 1024), 1024)
                return total + lax.dot_general(
                    Z[mine, cols], A[rows, cols], (((1,), (1,)), ((), ())), preferred_element_type=F32
                )

            output = lax.fori_loop(0, D // 1024, along, jnp.zeros((chunk, 256), F32))
            E[:, rows] = ((output * SCALE - Tt[goals, rows]) * (1.0 / ALL)).astype(BF16)
            return 0

        lax.fori_loop(0, ALL // 256, errors, 0)

        def update(i, _):
            cols = pl.ds(pl.multiple_of(i * 512, 512), 512)
            grad = jnp.dot(E[...], A[:, cols], preferred_element_type=F32) * SCALE
            before = G[mine, cols]
            moment = 0.09 * before + 0.1 * grad
            second = 0.0475 * before * before + 0.05 * grad * grad
            step = moment * (1.0 / 0.19) / (jnp.sqrt(second * (1.0 / 0.0975)) + 1e-4)
            Hv[mine, cols] = (Pv[mine, cols].astype(F32) - 0.08 * step).astype(BF16)
            return 0

        lax.fori_loop(0, D // 512, update, 0)

    def straight(lo, hi):
        return send(Hv.at[pl.ds(lo, hi - lo)], Arr.at[pl.ds(lo, hi - lo)], (push.to, f))

    chunk_of(0)
    if back:
        leg = send(Hv.at[pl.ds(0, back)], relay.at[0], (push.next, f))
    first = straight(back, chunk)
    chunk_of(1)
    second = straight(chunk, 240)
    third = straight(240, ROWS)
    if back:
        leg.wait_recv()
        leg = send(relay.at[0], relay.at[1], (push.next, f))
        leg.wait_recv()
        leg = send(relay.at[1], Arr.at[pl.ds(0, back)], (push.end, f))

    saves = []

    def settle(lo, hi):
        def average(i, _):
            rows = pl.ds(pl.multiple_of(lo + i * 16, 16), 16)
            Pv[rows, :] = (0.5 * (Hv[rows, :].astype(F32) + Arr[rows, :].astype(F32))).astype(BF16)
            return 0

        lax.fori_loop(0, (hi - lo) // 16, average, 0)
        rows = pl.ds(lo, hi - lo)
        save = pltpu.make_async_copy(Pv.at[rows], out_ref.at[rows], local.at[len(saves)])
        save.start()
        saves.append(save)

    first.wait_recv()
    settle(back, chunk)
    second.wait_recv()
    settle(chunk, 240)
    third.wait_recv()
    settle(240, ROWS)
    if back:
        leg.wait_recv()
        settle(0, back)
    weight.wait_recv()
    wout_ref[...] = 0.5 * (W[...] + Warr[...])
    for save in saves:
        save.wait()
    send.finish()


def second_step(code, halfway, arrived, weight, warrived, a1, t1, grad):
    any_space = pl.BlockSpec(memory_space=pl.ANY)
    vmem = pl.BlockSpec(memory_space=pltpu.VMEM)
    return pl.pallas_call(
        functools.partial(second_kernel, code),
        out_shape=(jax.ShapeDtypeStruct((ROWS, D), BF16), jax.ShapeDtypeStruct((8, 128), F32)),
        in_specs=[any_space, any_space, vmem, vmem, any_space, any_space, any_space],
        out_specs=(any_space, vmem),
        scratch_shapes=[
            pltpu.VMEM((ALL, D), BF16),
            pltpu.VMEM((ROWS, D), BF16),
            pltpu.VMEM((ROWS, D), BF16),
            pltpu.VMEM((ROWS, D), BF16),
            pltpu.VMEM((ROWS, D), BF16),
            pltpu.VMEM((ROWS, D), F32),
            pltpu.VMEM((ALL, WIN), BF16),
            pltpu.VMEM((WIN, ALL), F32),
            pltpu.VMEM((160, ALL), BF16),
            pltpu.VMEM((8, 128), F32),
            pltpu.VMEM((8, 128), F32),
            pltpu.VMEM((2, 80, D), BF16),
            pltpu.SemaphoreType.DMA((8,)),
            pltpu.SemaphoreType.DMA((8,)),
            pltpu.SemaphoreType.DMA((6,)),
        ],
        compiler_params=pltpu.CompilerParams(
            collective_id=9 + code, has_side_effects=True, vmem_limit_bytes=VMEM_LIMIT
        ),
        name="second_step",
    )(halfway, arrived, weight, warrived, a1, t1, grad)


def per_device(activations, targets, params, push_weight, peer_codes):
    weight = jnp.broadcast_to(push_weight.astype(F32), (8, 128))
    halfway, grad, a1z, t1 = first_step(params[0], weight, activations, targets, 32)
    arrived, warrived, a1 = lax.switch(
        peer_codes[0], [functools.partial(exchange, code) for code in range(8)],
        halfway, weight, activations, a1z,
    )
    new, wnew = lax.switch(
        peer_codes[1], [functools.partial(second_step, code) for code in range(8)],
        halfway, arrived, weight, warrived, a1, t1, grad,
    )
    return new[None], wnew[0, :1].astype(BF16)


def solution(mesh):
    in_specs = (
        P(None, "rep", "fsdp", None),
        P(None, "rep", "fsdp", None),
        P("rep", "fsdp", None),
        P("rep"),
        P(),
    )
    return jax.shard_map(
        per_device, mesh=mesh, in_specs=in_specs, out_specs=(P("rep", "fsdp", None), P("rep")), check_vma=False
    )
```

```python
import functools

import jax
import jax.numpy as jnp
from jax import lax
from jax.experimental import pallas as pl
from jax.experimental.pallas import tpu as pltpu
from jax.sharding import PartitionSpec as P

MESH = pl.DeviceIdType.MESH
REPS, XS, ZS, YS = 32, 4, 2, 4
TOK, D, HW, ROWS = 128, 5120, 2560, 320
ALL = 1024
SCALE = D**-0.5
WIN = 384
F32, BF16 = jnp.float32, jnp.bfloat16
SLOT = {(0, 0): 0, (0, 1): 1, (-1, 0): 2, (1, 0): 3, (-1, 1): 4, (1, 1): 5, (2, 0): 6, (2, 1): 7}
CHUNK = 160
VMEM_LIMIT = 63 * 1024 * 1024


def place():
    return lax.axis_index("rep"), lax.axis_index("fsdp")


def member(f, dx, dz):
    x, z = lax.rem(f, XS), f // XS
    return lax.rem(z + dz, ZS) * XS + lax.rem(x + dx + XS, XS)


def moved(r, dy, dz):
    y, z, c = r // 8, lax.rem(r // 2, 4), lax.rem(r, 2)
    return lax.rem(y + dy + 8, 4) * 8 + lax.rem(z + dz + 8, 4) * 2 + c


def greet(devices):
    barrier = pltpu.get_barrier_semaphore()
    for device in devices:
        pl.semaphore_signal(barrier, inc=1, device_id=device, device_id_type=MESH)
    pl.semaphore_wait(barrier, len(devices))


class Sender:
    def __init__(self, send_sems, recv_sems):
        self.send_sems, self.recv_sems, self.used, self.started = send_sems, recv_sems, 0, []
        self.index = {}

    def make(self, src, dst, device, like=None):
        i = self.used if like is None else self.index[id(like)][0]
        if like is None:
            self.used += 1
        copy = pltpu.make_async_remote_copy(
            src_ref=src, dst_ref=dst, send_sem=self.send_sems.at[i], recv_sem=self.recv_sems.at[i],
            device_id=device, device_id_type=MESH,
        )
        self.index[id(copy)] = (i, copy)
        return copy

    def __call__(self, src, dst, device):
        copy = self.make(src, dst, device)
        copy.start()
        self.started.append(copy)
        return copy

    def finish(self):
        for copy in self.started:
            copy.wait_send()


def part(ref, slot, lo, hi):
    return ref.at[pl.ds(slot * TOK + lo, hi - lo)]


def target_window(f):
    return pl.ds(pl.multiple_of(320 * f - 64 * lax.rem(f, 2), 128), WIN)


def send_targets(sender, r, f, src, dst):
    copies = []
    for (dx, dz), _ in SLOT.items():
        if (dx, dz) == (0, 0):
            continue
        to = member(f, dx, dz)
        back = SLOT[(dx if dx == 2 else -dx, dz)]
        copies.append((back, sender(src.at[:, target_window(to)], part(dst, back, 0, TOK), (r, to))))
    return [copy for _, copy in sorted(copies, key=lambda c: c[0])]


def first_kernel(cut, p_ref, w_ref, act_ref, tgt_ref, h_ref, g_ref, a1z_ref, t1_ref,
                 A, Pv, Z, G, T, Tt, send_sems, recv_sems, local):
    r, f = place()
    right, left, across = (r, member(f, 1, 0)), (r, member(f, -1, 0)), (r, member(f, 0, 1))
    act0, act1 = act_ref.at[0, 0], act_ref.at[1, 0]
    load_p = pltpu.make_async_copy(p_ref, Pv, local.at[0])
    load_p.start()
    load_a = pltpu.make_async_copy(act0, part(A, 0, 0, TOK), local.at[1])
    load_a.start()
    load_t = pltpu.make_async_copy(tgt_ref.at[0, 0, :, target_window(f)], part(T, 0, 0, TOK), local.at[2])
    load_t.start()
    load_t1 = pltpu.make_async_copy(tgt_ref.at[1, 0, :, target_window(f)], part(t1_ref, 0, 0, TOK), local.at[3])
    load_t1.start()
    greet([(r, member(f, dx, dz)) for dx, dz in SLOT if (dx, dz) != (0, 0)])
    send = Sender(send_sems, recv_sems)

    def own(lo, hi, slot, device):
        return send(act0.at[pl.ds(lo, hi - lo)], part(A, slot, lo, hi), device)

    def forward(source, slot, lo, hi, device):
        return send(part(A, source, lo, hi), part(A, slot, lo, hi), device)

    half = cut + (TOK - cut) // 32 * 16
    z_low = own(cut, TOK, 1, across)
    x_right = own(0, TOK, 2, right)
    x_left = own(0, TOK, 3, left)
    z_top = own(0, cut, 1, across)
    early = send(act1, a1z_ref, across)
    t_copies = send_targets(send, r, f, tgt_ref.at[0, 0], T)

    load_p.wait()
    inverse = 1.0 / w_ref[0:1, 0:1]

    def debias(i, _):
        rows = pl.ds(pl.multiple_of(i * 32, 32), 32)
        Z[rows, :] = (Pv[rows, :].astype(F32) * inverse).astype(BF16)
        return 0

    lax.fori_loop(0, ROWS // 32, debias, 0)

    def use_pair(k):
        rows = pl.ds(k * 2 * TOK, 2 * TOK)
        Tt[...] = T[rows, :].astype(F32).T
        goal = Tt[pl.ds(pl.multiple_of(64 * lax.rem(f, 2), 64), ROWS), :]

        output = lax.dot_general(Z[...], A[rows, :], (((1,), (1,)), ((), ())), preferred_element_type=F32)
        error = ((output * SCALE - goal) * (1.0 / ALL)).astype(BF16)

        def grad(i, _):
            cols = pl.ds(pl.multiple_of(i * 1024, 1024), 1024)
            new = jnp.dot(error, A[rows, cols], preferred_element_type=F32)
            if k == 0:
                G[:, cols] = new
            elif k < 3:
                G[:, cols] += new
            else:
                total = (G[:, cols] + new) * SCALE
                G[:, cols] = total
            return 0

        lax.fori_loop(0, D // 1024, grad, 0)

    z_low.wait_recv()
    b_right = forward(1, 4, cut, TOK, right)
    b_left = forward(1, 5, cut, TOK, left)
    x_right.wait_recv()
    f_right = forward(2, 6, 0, 64, right)
    z_2 = forward(2, 4, 0, cut, across)
    x_left.wait_recv()
    f_left = forward(3, 6, 64, TOK, left)
    z_3 = forward(3, 5, 0, cut, across)
    z_top.wait_recv()
    load_a.wait()
    load_t.wait()
    t_copies[0].wait_recv()
    use_pair(0)
    b_right.wait_recv()
    g_right = forward(4, 7, cut, half, right)
    b_left.wait_recv()
    g_left = forward(5, 7, half, TOK, left)
    t_copies[1].wait_recv()
    t_copies[2].wait_recv()
    use_pair(1)
    f_right.wait_recv()
    z_6 = forward(6, 7, 0, cut, across)
    z_2.wait_recv()
    z_3.wait_recv()
    t_copies[3].wait_recv()
    t_copies[4].wait_recv()
    use_pair(2)
    f_left.wait_recv()
    g_right.wait_recv()
    g_left.wait_recv()
    z_6.wait_recv()
    t_copies[5].wait_recv()
    t_copies[6].wait_recv()
    t1_copies = send_targets(send, r, f, tgt_ref.at[1, 0], t1_ref)
    use_pair(3)
    save_g = pltpu.make_async_copy(G, g_ref, local.at[0])
    save_g.start()

    def update(i, _):
        rows = pl.ds(pl.multiple_of(i * 16, 16), 16)
        grad = G[rows, :]
        Z[rows, :] = (Pv[rows, :].astype(F32) - 0.08 * (grad / (jnp.abs(grad) + 1e-4))).astype(BF16)
        return 0

    lax.fori_loop(0, ROWS // 16, update, 0)
    save_h = pltpu.make_async_copy(Z, h_ref, local.at[1])
    save_h.start()
    early.wait_recv()
    for copy in t1_copies:
        copy.wait_recv()
    load_t1.wait()
    save_g.wait()
    save_h.wait()
    send.finish()


def first_step(params, weight, activations, targets, cut):
    any_space = pl.BlockSpec(memory_space=pl.ANY)
    return pl.pallas_call(
        functools.partial(first_kernel, cut),
        out_shape=(
            jax.ShapeDtypeStruct((ROWS, D), BF16),
            jax.ShapeDtypeStruct((ROWS, D), F32),
            jax.ShapeDtypeStruct((TOK, D), BF16),
            jax.ShapeDtypeStruct((ALL, WIN), BF16),
        ),
        in_specs=[any_space, pl.BlockSpec(memory_space=pltpu.VMEM), any_space, any_space],
        out_specs=(any_space,) * 4,
        scratch_shapes=[
            pltpu.VMEM((ALL, D), BF16),
            pltpu.VMEM((ROWS, D), BF16),
            pltpu.VMEM((ROWS, D), BF16),
            pltpu.VMEM((ROWS, D), F32),
            pltpu.VMEM((ALL, WIN), BF16),
            pltpu.VMEM((WIN, 2 * TOK), F32),
            pltpu.SemaphoreType.DMA((32,)),
            pltpu.SemaphoreType.DMA((32,)),
            pltpu.SemaphoreType.DMA((4,)),
        ],
        compiler_params=pltpu.CompilerParams(
            collective_id=0, has_side_effects=True, vmem_limit_bytes=VMEM_LIMIT
        ),
        name="first_step",
    )(params, weight, activations, targets)


class Push:
    def __init__(self, code, r, f, send, relay):
        power = 1 << (code // 2)
        offset = power if code % 2 == 0 else -power
        self.f, self.send, self.relay = f, send, relay
        self.to, self.source = lax.rem(r + offset + REPS, REPS), lax.rem(r - offset + REPS, REPS)
        self.legs = code // 2 != 2
        self.back = 80 if self.legs else 0
        self.crosses = lax.rem(r, 2) == (1 if code == 0 else 0) if code < 2 else None
        if self.legs:
            way = -1 if code % 2 == 0 else 1
            dy, dz = (way, 0) if code // 2 == 3 else (0, way)
            self.next, self.last_one = moved(r, dy, dz), moved(r, -dy, -dz)
            self.end = lax.rem(moved(r, -2 * dy, -2 * dz) + offset + REPS, REPS)
            self.start_of_end = moved(self.source, 2 * dy, 2 * dz)

    def partners(self):
        both = [self.to, self.source]
        if self.legs:
            both += [self.next, self.last_one, self.end, self.start_of_end]
        return [(device, self.f) for device in both]

    def straight(self, src, dst):
        return self.send(src, dst, (self.to, self.f))

    def _crossing(self, act):
        if self.crosses is None:
            act()
        else:
            pl.when(self.crosses)(act)

    def first_leg(self, src, dst):
        relay = self.relay
        self.hops = [
            self.send.make(src, relay.at[0], (self.next, self.f)),
            self.send.make(relay.at[0], relay.at[1], (self.next, self.f)),
            self.send.make(relay.at[1], dst, (self.end, self.f)),
        ]
        self._crossing(self.hops[0].start)
        if self.crosses is not None:
            near = self.send.make(src, dst, (self.to, self.f), like=self.hops[2])
            pl.when(jnp.logical_not(self.crosses))(near.start)

    def next_leg(self, i):
        if not self.legs:
            return

        def act():
            self.hops[i - 1].wait_recv()
            self.hops[i].start()

        self._crossing(act)

    def arrived(self):
        if self.legs:
            self.hops[2].wait_recv()

    def finish(self):
        if self.legs:
            self._crossing(self.hops[0].wait_send)
            self._crossing(self.hops[1].wait_send)
            self.hops[2].wait_send()


def over_tiles(height, work):
    def tile(i, _):
        work(pl.ds(pl.multiple_of(lax.div(i, 5) * 16, 16), 16), pl.ds(pl.multiple_of(lax.rem(i, 5) * 1024, 1024), 1024))
        return 0

    lax.fori_loop(0, height // 16 * 5, tile, 0)


def debias_rows(P_, Arr, Z, inverse):
    def average(rows, cols):
        new = (0.5 * (P_[rows, cols].astype(F32) + Arr[rows, cols].astype(F32))).astype(BF16)
        P_[rows, cols] = new
        Z[rows, cols] = (new.astype(F32) * inverse).astype(BF16)

    over_tiles(CHUNK, average)


def turn_targets(T, Tt):
    def turn(i, _):
        rows = pl.ds(pl.multiple_of(i * 256, 256), 256)
        Tt[:, rows] = T[rows, :].astype(F32).T
        return 0

    lax.fori_loop(0, ALL // 256, turn, 0)


def pair_errors(Z, A, Tt, E, goals, k):
    rows = pl.ds(pl.multiple_of(k * 256, 256), 256)

    def along(i, total):
        cols = pl.ds(pl.multiple_of(i * 1024, 1024), 1024)
        return total + lax.dot_general(
            Z[:, cols], A[rows, cols], (((1,), (1,)), ((), ())), preferred_element_type=F32
        )

    output = lax.fori_loop(0, D // 1024, along, jnp.zeros((CHUNK, 256), F32))
    E[:, rows] = ((output * SCALE - Tt[goals, rows]) * (1.0 / ALL)).astype(BF16)


def second_update(E, A, G, P_, H):
    def update(i, _):
        cols = pl.ds(pl.multiple_of(i * 512, 512), 512)
        grad = jnp.dot(E[...], A[:, cols], preferred_element_type=F32) * SCALE
        before = G[:, cols]
        moment = 0.09 * before + 0.1 * grad
        second = 0.0475 * before * before + 0.05 * grad * grad
        step = moment * (1.0 / 0.19) / (jnp.sqrt(second * (1.0 / 0.0975)) + 1e-4)
        H[:, cols] = (P_[:, cols].astype(F32) - 0.08 * step).astype(BF16)
        return 0

    lax.fori_loop(0, D // 512, update, 0)


def exchange_kernel(code, cut, h_ref, w_ref, act_ref, a1z_ref, t1_ref, g_ref,
                    h1_ref, arr_ref, w1_ref, a1_ref, tt_ref,
                    A, Pv, Z, Arr, G, T, Tt, E, W, Warr, relay, send_sems, recv_sems, local):
    r, f = place()
    right, left, across = (r, member(f, 1, 0)), (r, member(f, -1, 0)), (r, member(f, 0, 1))
    act1 = act_ref.at[1, 0]
    top = pl.ds(0, CHUNK)
    loads = []
    for src, dst in [
        (act1, part(A, 0, 0, TOK)), (a1z_ref, part(A, 1, 0, TOK)), (t1_ref, T),
        (h_ref.at[top], Pv), (g_ref.at[top], G), (w_ref, W),
    ]:
        loads.append(pltpu.make_async_copy(src, dst, local.at[len(loads)]))
        loads[-1].start()
    send = Sender(send_sems, recv_sems)
    push = Push(code, r, f, send, relay)
    greet([right, left] + ([across] if cut else []) + push.partners())

    def forward(source, slot, lo, hi, device):
        return send(part(A, source, lo, hi), part(A, slot, lo, hi), device)

    rest = ROWS - CHUNK - push.back
    if push.back:
        push.first_leg(h_ref.at[pl.ds(CHUNK + rest, push.back)], arr_ref.at[pl.ds(rest, push.back)])
    straight = [push.straight(h_ref.at[pl.ds(lo, hi - lo)], Arr.at[pl.ds(lo, hi - lo)]) for lo, hi in ((0, 112), (112, CHUNK))]
    weight = push.straight(w_ref, Warr)
    x_right = send(act1, part(A, 2, 0, TOK), right)
    x_left = send(act1, part(A, 3, 0, TOK), left)
    b_right = send(a1z_ref.at[pl.ds(cut, TOK - cut)], part(A, 4, cut, TOK), right)
    b_left = send(a1z_ref.at[pl.ds(cut, TOK - cut)], part(A, 5, cut, TOK), left)
    half = cut + (TOK - cut) // 32 * 16
    loads[2].wait()
    turn_targets(T, Tt)
    save_t = pltpu.make_async_copy(Tt, tt_ref, local.at[2])
    save_t.start()
    push.next_leg(1)
    x_right.wait_recv()
    f_right = forward(2, 6, 0, 64, right)
    x_left.wait_recv()
    f_left = forward(3, 6, 64, TOK, left)
    ups = []
    if cut:
        ups = [forward(2, 4, 0, cut, across), forward(3, 5, 0, cut, across)]
    b_right.wait_recv()
    g_right = forward(4, 7, cut, half, right)
    b_left.wait_recv()
    g_left = forward(5, 7, half, TOK, left)
    straight[0].wait_recv()
    straight.append(push.straight(h_ref.at[pl.ds(CHUNK, rest)], arr_ref.at[pl.ds(0, rest)]))
    push.next_leg(2)
    weight.wait_recv()
    straight[1].wait_recv()
    for load in loads[:2] + loads[3:]:
        load.wait()
    w1 = (0.5 * (W[...] + Warr[...])).astype(BF16).astype(F32)
    w1_ref[...] = w1
    debias_rows(Pv, Arr, Z, 1.0 / w1[0:1, 0:1])
    goals = pl.ds(pl.multiple_of(64 * lax.rem(f, 2), 64), CHUNK)
    if cut:
        ups.append(send.make(part(A, 6, 0, cut), part(A, 7, 0, cut), across))
        send.started.append(ups[2])

    def errors(k, _):
        @pl.when(k == 2)
        def _():
            f_right.wait_recv()
            if cut:
                ups[2].start()
                ups[0].wait_recv()
                ups[1].wait_recv()

        @pl.when(k == 3)
        def _():
            f_left.wait_recv()
            g_right.wait_recv()
            g_left.wait_recv()
            if cut:
                ups[2].wait_recv()

        pair_errors(Z, A, Tt, E, goals, k)
        return 0

    lax.fori_loop(0, ALL // 256, errors, 0)
    save_a = pltpu.make_async_copy(A, a1_ref, local.at[0])
    save_a.start()
    second_update(E, A, G, Pv, Arr)
    save_h = pltpu.make_async_copy(Arr, h1_ref, local.at[1])
    save_h.start()
    straight[2].wait_recv()
    push.arrived()
    save_a.wait()
    save_h.wait()
    save_t.wait()
    send.finish()
    push.finish()


def exchange(code, halfway, weight, activations, a1z, t1, grad):
    any_space = pl.BlockSpec(memory_space=pl.ANY)
    vmem = pl.BlockSpec(memory_space=pltpu.VMEM)
    return pl.pallas_call(
        functools.partial(exchange_kernel, code, (32, 0, 0, 64)[code // 2]),
        out_shape=(
            jax.ShapeDtypeStruct((CHUNK, D), BF16),
            jax.ShapeDtypeStruct((ROWS - CHUNK, D), BF16),
            jax.ShapeDtypeStruct((8, 128), F32),
            jax.ShapeDtypeStruct((ALL, D), BF16),
            jax.ShapeDtypeStruct((WIN, ALL), F32),
        ),
        in_specs=[any_space] * 6,
        out_specs=(any_space, any_space, vmem, any_space, any_space),
        scratch_shapes=[
            pltpu.VMEM((ALL, D), BF16),
            pltpu.VMEM((CHUNK, D), BF16),
            pltpu.VMEM((CHUNK, D), BF16),
            pltpu.VMEM((CHUNK, D), BF16),
            pltpu.VMEM((CHUNK, D), F32),
            pltpu.VMEM((ALL, WIN), BF16),
            pltpu.VMEM((WIN, ALL), F32),
            pltpu.VMEM((CHUNK, ALL), BF16),
            pltpu.VMEM((8, 128), F32),
            pltpu.VMEM((8, 128), F32),
            pltpu.VMEM((2, 80, D), BF16),
            pltpu.SemaphoreType.DMA((20,)),
            pltpu.SemaphoreType.DMA((20,)),
            pltpu.SemaphoreType.DMA((6,)),
        ],
        compiler_params=pltpu.CompilerParams(
            collective_id=1 + code, has_side_effects=True, vmem_limit_bytes=VMEM_LIMIT
        ),
        name="exchange",
    )(halfway, weight, activations, a1z, t1, grad)


def second_kernel(code, h1_ref, h_ref, arr_ref, w1_ref, a1_ref, tt_ref, g_ref, out_ref, wout_ref,
                  A, Pv, Z, Hv, Hlow, Arr, G, Tt, E, W, Warr, relay, send_sems, recv_sems, local):
    r, f = place()
    low = pl.ds(CHUNK, ROWS - CHUNK)
    loads = []
    for src, dst in [
        (tt_ref, Tt), (h_ref.at[low], Pv), (arr_ref, Hlow), (a1_ref, A), (g_ref.at[low], G), (h1_ref, Hv),
    ]:
        loads.append(pltpu.make_async_copy(src, dst, local.at[len(loads)]))
        loads[-1].start()
    send = Sender(send_sems, recv_sems)
    push = Push(code, r, f, send, relay)
    back = push.back
    W[...] = w1_ref[...]
    greet(push.partners())
    if back:
        push.first_leg(h1_ref.at[pl.ds(0, back)], Arr.at[pl.ds(0, back)])
    first = push.straight(h1_ref.at[pl.ds(back, CHUNK - back)], Arr.at[pl.ds(back, CHUNK - back)])
    weight = push.straight(W, Warr)
    loads[0].wait()
    loads[1].wait()
    loads[2].wait()
    debias_rows(Pv, Hlow, Z, 1.0 / W[0:1, 0:1])
    loads[3].wait()
    goals = pl.ds(pl.multiple_of(CHUNK + 64 * lax.rem(f, 2), 32), CHUNK)

    def errors(k, _):
        pair_errors(Z, A, Tt, E, goals, k)
        return 0

    lax.fori_loop(0, ALL // 256, errors, 0)
    loads[4].wait()
    second_update(E, A, G, Pv, Hlow)
    cut = 80
    second = push.straight(Hlow.at[pl.ds(0, cut)], Arr.at[pl.ds(CHUNK, cut)])
    third = push.straight(Hlow.at[pl.ds(cut, CHUNK - cut)], Arr.at[pl.ds(CHUNK + cut, CHUNK - cut)])
    push.next_leg(1)
    loads[5].wait()
    saves = []

    def settle(lo, hi):
        source, shift = (Hv, 0) if lo < CHUNK else (Hlow, CHUNK)

        own, other = source.at[pl.ds(lo - shift, hi - lo)], Arr.at[pl.ds(lo, hi - lo)]

        def average(rows, cols):
            new = 0.5 * (own[rows, cols].astype(F32) + other[rows, cols].astype(F32))
            other[rows, cols] = new.astype(BF16)

        over_tiles(hi - lo, average)
        rows = pl.ds(lo, hi - lo)
        save = pltpu.make_async_copy(Arr.at[rows], out_ref.at[rows], local.at[len(saves)])
        save.start()
        saves.append(save)

    first.wait_recv()
    settle(back, CHUNK)
    push.next_leg(2)
    second.wait_recv()
    settle(CHUNK, CHUNK + cut)
    weight.wait_recv()
    wout_ref[...] = 0.5 * (W[...] + Warr[...])
    third.wait_recv()
    settle(CHUNK + cut, ROWS)
    if back:
        push.arrived()
        settle(0, back)
    send.finish()
    push.finish()
    for save in saves:
        save.wait()


def second_step(code, h1, halfway, arrived, weight, a1, tt, grad):
    any_space = pl.BlockSpec(memory_space=pl.ANY)
    vmem = pl.BlockSpec(memory_space=pltpu.VMEM)
    return pl.pallas_call(
        functools.partial(second_kernel, code),
        out_shape=(jax.ShapeDtypeStruct((ROWS, D), BF16), jax.ShapeDtypeStruct((8, 128), F32)),
        in_specs=[any_space, any_space, any_space, vmem, any_space, any_space, any_space],
        out_specs=(any_space, vmem),
        scratch_shapes=[
            pltpu.VMEM((ALL, D), BF16),
            pltpu.VMEM((CHUNK, D), BF16),
            pltpu.VMEM((CHUNK, D), BF16),
            pltpu.VMEM((CHUNK, D), BF16),
            pltpu.VMEM((CHUNK, D), BF16),
            pltpu.VMEM((ROWS, D), BF16),
            pltpu.VMEM((CHUNK, D), F32),
            pltpu.VMEM((WIN, ALL), F32),
            pltpu.VMEM((CHUNK, ALL), BF16),
            pltpu.VMEM((8, 128), F32),
            pltpu.VMEM((8, 128), F32),
            pltpu.VMEM((2, 80, D), BF16),
            pltpu.SemaphoreType.DMA((8,)),
            pltpu.SemaphoreType.DMA((8,)),
            pltpu.SemaphoreType.DMA((6,)),
        ],
        compiler_params=pltpu.CompilerParams(
            collective_id=9 + code, has_side_effects=True, vmem_limit_bytes=VMEM_LIMIT - 7 * 1024 * 1024
        ),
        name="second_step",
    )(h1, halfway, arrived, weight, a1, tt, grad)


def per_device(activations, targets, params, push_weight, peer_codes):
    weight = jnp.broadcast_to(push_weight.astype(F32), (8, 128))
    halfway, grad, a1z, t1 = first_step(params[0], weight, activations, targets, 32)
    h1, arrived, weight, a1, tt = lax.switch(
        peer_codes[0], [functools.partial(exchange, code) for code in range(8)],
        halfway, weight, activations, a1z, t1, grad,
    )
    new, wnew = lax.switch(
        peer_codes[1], [functools.partial(second_step, code) for code in range(8)],
        h1, halfway, arrived, weight, a1, tt, grad,
    )
    return new[None], wnew[0, :1].astype(BF16)


def solution(mesh):
    in_specs = (
        P(None, "rep", "fsdp", None),
        P(None, "rep", "fsdp", None),
        P("rep", "fsdp", None),
        P("rep"),
        P(),
    )
    return jax.shard_map(
        per_device, mesh=mesh, in_specs=in_specs, out_specs=(P("rep", "fsdp", None), P("rep")), check_vma=False
    )
```

```python
import functools

import jax
import jax.numpy as jnp
from jax import lax
from jax.experimental import pallas as pl
from jax.experimental.pallas import tpu as pltpu
from jax.sharding import PartitionSpec as P

MESH = pl.DeviceIdType.MESH
REPS, XS, ZS, YS = 32, 4, 2, 4
TOK, D, HW, ROWS = 128, 5120, 2560, 320
ALL = 1024
SCALE = D**-0.5
F32, BF16 = jnp.float32, jnp.bfloat16
SLOT = {(0, 0): 0, (0, 1): 1, (-1, 0): 2, (1, 0): 3, (-1, 1): 4, (1, 1): 5, (2, 0): 6, (2, 1): 7}
CHUNK = 160
VMEM_LIMIT = 63 * 1024 * 1024


def place():
    return lax.axis_index("rep"), lax.axis_index("fsdp")


def member(f, dx, dz):
    x, z = lax.rem(f, XS), f // XS
    return lax.rem(z + dz, ZS) * XS + lax.rem(x + dx + XS, XS)


def moved(r, dy, dz):
    y, z, c = r // 8, lax.rem(r // 2, 4), lax.rem(r, 2)
    return lax.rem(y + dy + 8, 4) * 8 + lax.rem(z + dz + 8, 4) * 2 + c


def greet(devices):
    barrier = pltpu.get_barrier_semaphore()
    for device in devices:
        pl.semaphore_signal(barrier, inc=1, device_id=device, device_id_type=MESH)
    pl.semaphore_wait(barrier, len(devices))


class Sender:
    def __init__(self, send_sems, recv_sems):
        self.send_sems, self.recv_sems, self.used, self.started = send_sems, recv_sems, 0, []
        self.index = {}

    def make(self, src, dst, device, like=None):
        i = self.used if like is None else self.index[id(like)][0]
        if like is None:
            self.used += 1
        copy = pltpu.make_async_remote_copy(
            src_ref=src, dst_ref=dst, send_sem=self.send_sems.at[i], recv_sem=self.recv_sems.at[i],
            device_id=device, device_id_type=MESH,
        )
        self.index[id(copy)] = (i, copy)
        return copy

    def __call__(self, src, dst, device):
        copy = self.make(src, dst, device)
        copy.start()
        self.started.append(copy)
        return copy

    def finish(self):
        for copy in self.started:
            copy.wait_send()


def part(ref, slot, lo, hi):
    return ref.at[pl.ds(slot * TOK + lo, hi - lo)]


def features_of(f):
    return pl.ds(pl.multiple_of(ROWS * f, 64), ROWS)


def transpose_targets(src, dst):
    def tile(i, _):
        block = pl.ds(pl.multiple_of(i * 128, 128), 128)
        dst[block, :] = src[:, block].astype(F32).T.astype(BF16)
        return 0

    lax.fori_loop(0, HW // 128, tile, 0)


def send_targets(sender, r, f, src, dst):
    copies = []
    for dx, dz in SLOT:
        if (dx, dz) == (0, 0):
            continue
        to = member(f, dx, dz)
        back = SLOT[(dx if dx == 2 else -dx, dz)]
        copies.append((back, sender(src.at[features_of(to)], dst.at[back], (r, to))))
    return [copy for _, copy in sorted(copies, key=lambda c: c[0])]


def first_kernel(cut, p_ref, w_ref, act_ref, tgt_ref, h_ref, g_ref, a1z_ref, t1_ref,
                 A, Pv, Z, G, T, raw0, raw1, turned0, turned1, send_sems, recv_sems, local):
    r, f = place()
    right, left, across = (r, member(f, 1, 0)), (r, member(f, -1, 0)), (r, member(f, 0, 1))
    act0, act1 = act_ref.at[0, 0], act_ref.at[1, 0]
    load_p = pltpu.make_async_copy(p_ref, Pv, local.at[0])
    load_p.start()
    load_a = pltpu.make_async_copy(act0, part(A, 0, 0, TOK), local.at[1])
    load_a.start()
    load_t0 = pltpu.make_async_copy(tgt_ref.at[0, 0], raw0, local.at[2])
    load_t0.start()
    load_t1 = pltpu.make_async_copy(tgt_ref.at[1, 0], raw1, local.at[3])
    load_t1.start()
    greet([(r, member(f, dx, dz)) for dx, dz in SLOT if (dx, dz) != (0, 0)])
    send = Sender(send_sems, recv_sems)

    def own(lo, hi, slot, device):
        return send(act0.at[pl.ds(lo, hi - lo)], part(A, slot, lo, hi), device)

    def forward(source, slot, lo, hi, device):
        return send(part(A, source, lo, hi), part(A, slot, lo, hi), device)

    half = cut + (TOK - cut) // 32 * 16
    z_low = own(cut, TOK, 1, across)
    x_right = own(0, TOK, 2, right)
    x_left = own(0, TOK, 3, left)
    z_top = own(0, cut, 1, across)
    early = send(act1, a1z_ref, across)
    load_t0.wait()
    transpose_targets(raw0, turned0)
    t_copies = send_targets(send, r, f, turned0, T)
    own_t0 = pltpu.make_async_copy(turned0.at[features_of(f)], T.at[0], local.at[4])
    own_t0.start()
    load_t1.wait()
    transpose_targets(raw1, turned1)
    own_t1 = pltpu.make_async_copy(turned1.at[features_of(f)], t1_ref.at[0], local.at[5])
    own_t1.start()

    load_p.wait()
    inverse = 1.0 / w_ref[0:1, 0:1]

    def debias(i, _):
        rows = pl.ds(pl.multiple_of(i * 32, 32), 32)
        Z[rows, :] = (Pv[rows, :].astype(F32) * inverse).astype(BF16)
        return 0

    lax.fori_loop(0, ROWS // 32, debias, 0)

    def use_pair(k):
        rows = pl.ds(k * 2 * TOK, 2 * TOK)
        goal = jnp.concatenate([T[2 * k], T[2 * k + 1]], axis=1).astype(F32)

        output = lax.dot_general(Z[...], A[rows, :], (((1,), (1,)), ((), ())), preferred_element_type=F32)
        error = ((output * SCALE - goal) * (1.0 / ALL)).astype(BF16)

        def grad(i, _):
            cols = pl.ds(pl.multiple_of(i * 1024, 1024), 1024)
            new = jnp.dot(error, A[rows, cols], preferred_element_type=F32)
            if k == 0:
                G[:, cols] = new
            elif k < 3:
                G[:, cols] += new
            else:
                total = (G[:, cols] + new) * SCALE
                G[:, cols] = total
            return 0

        lax.fori_loop(0, D // 1024, grad, 0)

    z_low.wait_recv()
    b_right = forward(1, 4, cut, TOK, right)
    b_left = forward(1, 5, cut, TOK, left)
    x_right.wait_recv()
    f_right = forward(2, 6, 0, 64, right)
    z_2 = forward(2, 4, 0, cut, across)
    x_left.wait_recv()
    f_left = forward(3, 6, 64, TOK, left)
    z_3 = forward(3, 5, 0, cut, across)
    z_top.wait_recv()
    load_a.wait()
    own_t0.wait()
    t_copies[0].wait_recv()
    use_pair(0)
    b_right.wait_recv()
    g_right = forward(4, 7, cut, half, right)
    b_left.wait_recv()
    g_left = forward(5, 7, half, TOK, left)
    t_copies[1].wait_recv()
    t_copies[2].wait_recv()
    use_pair(1)
    f_right.wait_recv()
    z_6 = forward(6, 7, 0, cut, across)
    z_2.wait_recv()
    z_3.wait_recv()
    t_copies[3].wait_recv()
    t_copies[4].wait_recv()
    use_pair(2)
    f_left.wait_recv()
    g_right.wait_recv()
    g_left.wait_recv()
    z_6.wait_recv()
    t_copies[5].wait_recv()
    t_copies[6].wait_recv()
    t1_copies = send_targets(send, r, f, turned1, t1_ref)
    use_pair(3)
    save_g = pltpu.make_async_copy(G, g_ref, local.at[0])
    save_g.start()

    def update(i, _):
        rows = pl.ds(pl.multiple_of(i * 16, 16), 16)
        grad = G[rows, :]
        Z[rows, :] = (Pv[rows, :].astype(F32) - 0.08 * (grad / (jnp.abs(grad) + 1e-4))).astype(BF16)
        return 0

    lax.fori_loop(0, ROWS // 16, update, 0)
    save_h = pltpu.make_async_copy(Z, h_ref, local.at[1])
    save_h.start()
    early.wait_recv()
    for copy in t1_copies:
        copy.wait_recv()
    own_t1.wait()
    save_g.wait()
    save_h.wait()
    send.finish()


def first_step(params, weight, activations, targets, cut):
    any_space = pl.BlockSpec(memory_space=pl.ANY)
    return pl.pallas_call(
        functools.partial(first_kernel, cut),
        out_shape=(
            jax.ShapeDtypeStruct((ROWS, D), BF16),
            jax.ShapeDtypeStruct((ROWS, D), F32),
            jax.ShapeDtypeStruct((TOK, D), BF16),
            jax.ShapeDtypeStruct((8, ROWS, TOK), BF16),
        ),
        in_specs=[any_space, pl.BlockSpec(memory_space=pltpu.VMEM), any_space, any_space],
        out_specs=(any_space,) * 4,
        scratch_shapes=[
            pltpu.VMEM((ALL, D), BF16),
            pltpu.VMEM((ROWS, D), BF16),
            pltpu.VMEM((ROWS, D), BF16),
            pltpu.VMEM((ROWS, D), F32),
            pltpu.VMEM((8, ROWS, TOK), BF16),
            pltpu.VMEM((TOK, HW), BF16),
            pltpu.VMEM((TOK, HW), BF16),
            pltpu.VMEM((HW, TOK), BF16),
            pltpu.VMEM((HW, TOK), BF16),
            pltpu.SemaphoreType.DMA((32,)),
            pltpu.SemaphoreType.DMA((32,)),
            pltpu.SemaphoreType.DMA((6,)),
        ],
        compiler_params=pltpu.CompilerParams(
            collective_id=0, has_side_effects=True, vmem_limit_bytes=VMEM_LIMIT
        ),
        name="first_step",
    )(params, weight, activations, targets)


class Push:
    def __init__(self, code, r, f, send, relay):
        power = 1 << (code // 2)
        offset = power if code % 2 == 0 else -power
        self.f, self.send, self.relay = f, send, relay
        self.to, self.source = lax.rem(r + offset + REPS, REPS), lax.rem(r - offset + REPS, REPS)
        self.legs = code // 2 != 2
        self.back = 80 if self.legs else 0
        self.crosses = lax.rem(r, 2) == (1 if code == 0 else 0) if code < 2 else None
        if self.legs:
            way = -1 if code % 2 == 0 else 1
            dy, dz = (way, 0) if code // 2 == 3 else (0, way)
            self.next, self.last_one = moved(r, dy, dz), moved(r, -dy, -dz)
            self.end = lax.rem(moved(r, -2 * dy, -2 * dz) + offset + REPS, REPS)
            self.start_of_end = moved(self.source, 2 * dy, 2 * dz)

    def partners(self):
        both = [self.to, self.source]
        if self.legs:
            both += [self.next, self.last_one, self.end, self.start_of_end]
        return [(device, self.f) for device in both]

    def straight(self, src, dst):
        return self.send(src, dst, (self.to, self.f))

    def _crossing(self, act):
        if self.crosses is None:
            act()
        else:
            pl.when(self.crosses)(act)

    def first_leg(self, src, dst):
        relay = self.relay
        self.hops = [
            self.send.make(src, relay.at[0], (self.next, self.f)),
            self.send.make(relay.at[0], relay.at[1], (self.next, self.f)),
            self.send.make(relay.at[1], dst, (self.end, self.f)),
        ]
        self._crossing(self.hops[0].start)
        if self.crosses is not None:
            near = self.send.make(src, dst, (self.to, self.f), like=self.hops[2])
            pl.when(jnp.logical_not(self.crosses))(near.start)

    def next_leg(self, i):
        if not self.legs:
            return

        def act():
            self.hops[i - 1].wait_recv()
            self.hops[i].start()

        self._crossing(act)

    def arrived(self):
        if self.legs:
            self.hops[2].wait_recv()

    def finish(self):
        if self.legs:
            self._crossing(self.hops[0].wait_send)
            self._crossing(self.hops[1].wait_send)
            self.hops[2].wait_send()


def over_tiles(height, work):
    def tile(i, _):
        work(pl.ds(pl.multiple_of(lax.div(i, 5) * 16, 16), 16), pl.ds(pl.multiple_of(lax.rem(i, 5) * 1024, 1024), 1024))
        return 0

    lax.fori_loop(0, height // 16 * 5, tile, 0)


def debias_rows(P_, Arr, Z, inverse):
    def average(rows, cols):
        new = (0.5 * (P_[rows, cols].astype(F32) + Arr[rows, cols].astype(F32))).astype(BF16)
        P_[rows, cols] = new
        Z[rows, cols] = (new.astype(F32) * inverse).astype(BF16)

    over_tiles(CHUNK, average)


def pair_errors(Z, A, T, E, top, k):
    rows = pl.ds(pl.multiple_of(k * 256, 256), 256)

    def along(i, total):
        cols = pl.ds(pl.multiple_of(i * 1024, 1024), 1024)
        return total + lax.dot_general(
            Z[:, cols], A[rows, cols], (((1,), (1,)), ((), ())), preferred_element_type=F32
        )

    output = lax.fori_loop(0, D // 1024, along, jnp.zeros((CHUNK, 256), F32))
    mine = pl.ds(top, CHUNK)
    goal = jnp.concatenate([T[2 * k, mine, :], T[2 * k + 1, mine, :]], axis=1).astype(F32)
    E[:, rows] = ((output * SCALE - goal) * (1.0 / ALL)).astype(BF16)


def second_update(E, A, G, P_, H):
    def update(i, _):
        cols = pl.ds(pl.multiple_of(i * 512, 512), 512)
        grad = jnp.dot(E[...], A[:, cols], preferred_element_type=F32) * SCALE
        before = G[:, cols]
        moment = 0.09 * before + 0.1 * grad
        second = 0.0475 * before * before + 0.05 * grad * grad
        step = moment * (1.0 / 0.19) / (jnp.sqrt(second * (1.0 / 0.0975)) + 1e-4)
        H[:, cols] = (P_[:, cols].astype(F32) - 0.08 * step).astype(BF16)
        return 0

    lax.fori_loop(0, D // 512, update, 0)


def exchange_kernel(code, cut, h_ref, w_ref, act_ref, a1z_ref, t1_ref, g_ref,
                    h1_ref, arr_ref, w1_ref, a1_ref,
                    A, Pv, Z, Arr, G, T, E, W, Warr, relay, send_sems, recv_sems, local):
    r, f = place()
    right, left, across = (r, member(f, 1, 0)), (r, member(f, -1, 0)), (r, member(f, 0, 1))
    act1 = act_ref.at[1, 0]
    top = pl.ds(0, CHUNK)
    loads = []
    for src, dst in [
        (act1, part(A, 0, 0, TOK)), (a1z_ref, part(A, 1, 0, TOK)), (t1_ref, T),
        (h_ref.at[top], Pv), (g_ref.at[top], G), (w_ref, W),
    ]:
        loads.append(pltpu.make_async_copy(src, dst, local.at[len(loads)]))
        loads[-1].start()
    send = Sender(send_sems, recv_sems)
    push = Push(code, r, f, send, relay)
    greet([right, left] + ([across] if cut else []) + push.partners())

    def forward(source, slot, lo, hi, device):
        return send(part(A, source, lo, hi), part(A, slot, lo, hi), device)

    rest = ROWS - CHUNK - push.back
    if push.back:
        push.first_leg(h_ref.at[pl.ds(CHUNK + rest, push.back)], arr_ref.at[pl.ds(rest, push.back)])
    straight = [push.straight(h_ref.at[pl.ds(lo, hi - lo)], Arr.at[pl.ds(lo, hi - lo)]) for lo, hi in ((0, 112), (112, CHUNK))]
    weight = push.straight(w_ref, Warr)
    x_right = send(act1, part(A, 2, 0, TOK), right)
    x_left = send(act1, part(A, 3, 0, TOK), left)
    b_right = send(a1z_ref.at[pl.ds(cut, TOK - cut)], part(A, 4, cut, TOK), right)
    b_left = send(a1z_ref.at[pl.ds(cut, TOK - cut)], part(A, 5, cut, TOK), left)
    half = cut + (TOK - cut) // 32 * 16
    push.next_leg(1)
    x_right.wait_recv()
    f_right = forward(2, 6, 0, 64, right)
    x_left.wait_recv()
    f_left = forward(3, 6, 64, TOK, left)
    ups = []
    if cut:
        ups = [forward(2, 4, 0, cut, across), forward(3, 5, 0, cut, across)]
    b_right.wait_recv()
    g_right = forward(4, 7, cut, half, right)
    b_left.wait_recv()
    g_left = forward(5, 7, half, TOK, left)
    straight[0].wait_recv()
    straight.append(push.straight(h_ref.at[pl.ds(CHUNK, rest)], arr_ref.at[pl.ds(0, rest)]))
    push.next_leg(2)
    weight.wait_recv()
    straight[1].wait_recv()
    for load in loads:
        load.wait()
    w1 = (0.5 * (W[...] + Warr[...])).astype(BF16).astype(F32)
    w1_ref[...] = w1
    debias_rows(Pv, Arr, Z, 1.0 / w1[0:1, 0:1])
    if cut:
        ups.append(send.make(part(A, 6, 0, cut), part(A, 7, 0, cut), across))
        send.started.append(ups[2])

    def errors(k, _):
        @pl.when(k == 2)
        def _():
            f_right.wait_recv()
            if cut:
                ups[2].start()
                ups[0].wait_recv()
                ups[1].wait_recv()

        @pl.when(k == 3)
        def _():
            f_left.wait_recv()
            g_right.wait_recv()
            g_left.wait_recv()
            if cut:
                ups[2].wait_recv()

        pair_errors(Z, A, T, E, 0, k)
        return 0

    lax.fori_loop(0, ALL // 256, errors, 0)
    save_a = pltpu.make_async_copy(A, a1_ref, local.at[0])
    save_a.start()
    second_update(E, A, G, Pv, Arr)
    save_h = pltpu.make_async_copy(Arr, h1_ref, local.at[1])
    save_h.start()
    straight[2].wait_recv()
    push.arrived()
    save_a.wait()
    save_h.wait()
    send.finish()
    push.finish()


def exchange(code, halfway, weight, activations, a1z, t1, grad):
    any_space = pl.BlockSpec(memory_space=pl.ANY)
    vmem = pl.BlockSpec(memory_space=pltpu.VMEM)
    return pl.pallas_call(
        functools.partial(exchange_kernel, code, (32, 0, 0, 64)[code // 2]),
        out_shape=(
            jax.ShapeDtypeStruct((CHUNK, D), BF16),
            jax.ShapeDtypeStruct((ROWS - CHUNK, D), BF16),
            jax.ShapeDtypeStruct((8, 128), F32),
            jax.ShapeDtypeStruct((ALL, D), BF16),
        ),
        in_specs=[any_space] * 6,
        out_specs=(any_space, any_space, vmem, any_space),
        scratch_shapes=[
            pltpu.VMEM((ALL, D), BF16),
            pltpu.VMEM((CHUNK, D), BF16),
            pltpu.VMEM((CHUNK, D), BF16),
            pltpu.VMEM((CHUNK, D), BF16),
            pltpu.VMEM((CHUNK, D), F32),
            pltpu.VMEM((8, ROWS, TOK), BF16),
            pltpu.VMEM((CHUNK, ALL), BF16),
            pltpu.VMEM((8, 128), F32),
            pltpu.VMEM((8, 128), F32),
            pltpu.VMEM((2, 80, D), BF16),
            pltpu.SemaphoreType.DMA((20,)),
            pltpu.SemaphoreType.DMA((20,)),
            pltpu.SemaphoreType.DMA((6,)),
        ],
        compiler_params=pltpu.CompilerParams(
            collective_id=1 + code, has_side_effects=True, vmem_limit_bytes=VMEM_LIMIT
        ),
        name="exchange",
    )(halfway, weight, activations, a1z, t1, grad)


def second_kernel(code, h1_ref, h_ref, arr_ref, w1_ref, a1_ref, t1_ref, g_ref, out_ref, wout_ref,
                  A, Pv, Z, Hv, Hlow, Arr, G, T, E, W, Warr, relay, send_sems, recv_sems, local):
    r, f = place()
    low = pl.ds(CHUNK, ROWS - CHUNK)
    loads = []
    for src, dst in [
        (t1_ref, T), (h_ref.at[low], Pv), (arr_ref, Hlow), (a1_ref, A), (g_ref.at[low], G), (h1_ref, Hv),
    ]:
        loads.append(pltpu.make_async_copy(src, dst, local.at[len(loads)]))
        loads[-1].start()
    send = Sender(send_sems, recv_sems)
    push = Push(code, r, f, send, relay)
    back = push.back
    W[...] = w1_ref[...]
    greet(push.partners())
    if back:
        push.first_leg(h1_ref.at[pl.ds(0, back)], Arr.at[pl.ds(0, back)])
    first = push.straight(h1_ref.at[pl.ds(back, CHUNK - back)], Arr.at[pl.ds(back, CHUNK - back)])
    weight = push.straight(W, Warr)
    loads[0].wait()
    loads[1].wait()
    loads[2].wait()
    debias_rows(Pv, Hlow, Z, 1.0 / W[0:1, 0:1])
    loads[3].wait()

    def errors(k, _):
        pair_errors(Z, A, T, E, CHUNK, k)
        return 0

    lax.fori_loop(0, ALL // 256, errors, 0)
    loads[4].wait()
    second_update(E, A, G, Pv, Hlow)
    cut = 80
    second = push.straight(Hlow.at[pl.ds(0, cut)], Arr.at[pl.ds(CHUNK, cut)])
    third = push.straight(Hlow.at[pl.ds(cut, CHUNK - cut)], Arr.at[pl.ds(CHUNK + cut, CHUNK - cut)])
    push.next_leg(1)
    loads[5].wait()
    saves = []

    def settle(lo, hi):
        source, shift = (Hv, 0) if lo < CHUNK else (Hlow, CHUNK)

        own, other = source.at[pl.ds(lo - shift, hi - lo)], Arr.at[pl.ds(lo, hi - lo)]

        def average(rows, cols):
            new = 0.5 * (own[rows, cols].astype(F32) + other[rows, cols].astype(F32))
            other[rows, cols] = new.astype(BF16)

        over_tiles(hi - lo, average)
        rows = pl.ds(lo, hi - lo)
        save = pltpu.make_async_copy(Arr.at[rows], out_ref.at[rows], local.at[len(saves)])
        save.start()
        saves.append(save)

    first.wait_recv()
    settle(back, CHUNK)
    push.next_leg(2)
    second.wait_recv()
    settle(CHUNK, CHUNK + cut)
    weight.wait_recv()
    wout_ref[...] = 0.5 * (W[...] + Warr[...])
    third.wait_recv()
    settle(CHUNK + cut, ROWS)
    if back:
        push.arrived()
        settle(0, back)
    send.finish()
    push.finish()
    for save in saves:
        save.wait()


def second_step(code, h1, halfway, arrived, weight, a1, t1, grad):
    any_space = pl.BlockSpec(memory_space=pl.ANY)
    vmem = pl.BlockSpec(memory_space=pltpu.VMEM)
    return pl.pallas_call(
        functools.partial(second_kernel, code),
        out_shape=(jax.ShapeDtypeStruct((ROWS, D), BF16), jax.ShapeDtypeStruct((8, 128), F32)),
        in_specs=[any_space, any_space, any_space, vmem, any_space, any_space, any_space],
        out_specs=(any_space, vmem),
        scratch_shapes=[
            pltpu.VMEM((ALL, D), BF16),
            pltpu.VMEM((CHUNK, D), BF16),
            pltpu.VMEM((CHUNK, D), BF16),
            pltpu.VMEM((CHUNK, D), BF16),
            pltpu.VMEM((CHUNK, D), BF16),
            pltpu.VMEM((ROWS, D), BF16),
            pltpu.VMEM((CHUNK, D), F32),
            pltpu.VMEM((8, ROWS, TOK), BF16),
            pltpu.VMEM((CHUNK, ALL), BF16),
            pltpu.VMEM((8, 128), F32),
            pltpu.VMEM((8, 128), F32),
            pltpu.VMEM((2, 80, D), BF16),
            pltpu.SemaphoreType.DMA((8,)),
            pltpu.SemaphoreType.DMA((8,)),
            pltpu.SemaphoreType.DMA((6,)),
        ],
        compiler_params=pltpu.CompilerParams(
            collective_id=9 + code, has_side_effects=True, vmem_limit_bytes=VMEM_LIMIT - 7 * 1024 * 1024
        ),
        name="second_step",
    )(h1, halfway, arrived, weight, a1, t1, grad)


def per_device(activations, targets, params, push_weight, peer_codes):
    weight = jnp.broadcast_to(push_weight.astype(F32), (8, 128))
    halfway, grad, a1z, t1 = first_step(params[0], weight, activations, targets, 32)
    h1, arrived, weight, a1 = lax.switch(
        peer_codes[0], [functools.partial(exchange, code) for code in range(8)],
        halfway, weight, activations, a1z, t1, grad,
    )
    new, wnew = lax.switch(
        peer_codes[1], [functools.partial(second_step, code) for code in range(8)],
        h1, halfway, arrived, weight, a1, t1, grad,
    )
    return new[None], wnew[0, :1].astype(BF16)


def solution(mesh):
    in_specs = (
        P(None, "rep", "fsdp", None),
        P(None, "rep", "fsdp", None),
        P("rep", "fsdp", None),
        P("rep"),
        P(),
    )
    return jax.shard_map(
        per_device, mesh=mesh, in_specs=in_specs, out_specs=(P("rep", "fsdp", None), P("rep")), check_vma=False
    )
```
